32 devices in a mesh: grp: 2 (over x), wide: 16 (over z, y, core).
Axes of the slice: x: 2, y: 2, z: 4, core: 2. Of those that a mesh axis runs over, the one named last changes fastest.
Arguments:
- queries: bfloat16 [16384, 16384], P(('grp', 'wide')), parts along dimension 0, may hold values from -6 to 6
- train_rows: bfloat16 [1024, 16384], P(('grp', 'wide')), parts along dimension 0, may hold values from -0.015625 to 0.015625
- left_basis: bfloat16 [128, 128], replicated, may hold values from -0.5 to 0.5
- right_basis: bfloat16 [128, 128], replicated, may hold values from -0.5 to 0.5
- eigenvalues: float32 [128, 128], replicated, may hold values from 0.01 to 10
Outputs:
- scores: float32 [16384, 512], P(('grp', 'wide')), parts along dimension 0
The draws below stay inside these ranges and needn't reach their ends.
There are 2 independent parts, one for each index of `grp`. The reference program is written for one: setup_inputs(seed, part) draws one part's arguments, and reference() takes and returns one part's arrays. A program takes and returns all parts, laid end to end along the dimension named above; an argument that names none is the same for every part. Nothing has to cross between parts.
All inputs are finite; a program needn't handle non-finite values.
Results may differ from the reference program's by a relative error of at most 0.0049.
Values may be sent and summed in bfloat16 or wider, within the bound.
No kernel may reach another device: no remote copies, remote signals or barrier semaphores. Data moves between devices by JAX's collectives and lax.ppermute only.
A program may use at most 128 MiB of HBM per device.

```python
import math
import jax
import jax.numpy as jnp
from jax import lax

A_DIM = 128
B_DIM = 128
Q_DEV = 512
T_DEV = 32
PROJ = 16384
NQ = 8192
NT = 512


def level_of(rng, dims, pieces, smallest, top_value):
    gain = 1.0
    for dim, parts in pieces:
        steps = jax.random.uniform(jax.random.fold_in(jax.random.fold_in(rng, 6), dim), (parts,), jnp.float32, smallest / len(pieces), top_value / len(pieces))
        gain = gain * jnp.repeat(jnp.exp(steps), dims[dim] // parts).reshape((-1,) + (1,) * (len(dims) - 1 - dim))
    return gain


def normal_values(rng, dims, deviation, reach, split=(), kind=jnp.bfloat16):
    entries = deviation * jax.random.normal(rng, dims, jnp.float32)
    if split:
        entries = entries * level_of(rng, dims, split, -0.22, 0.18)
    return jnp.clip(entries, -reach, reach).astype(kind)


def setup_inputs(seed: int = 0, part: int = 0) -> dict:
    streams_of = jax.random.split(jax.random.key(seed), 6)
    part_keys = jax.random.split(jax.random.fold_in(streams_of[5], part), 6)
    queries = normal_values(part_keys[0], (NQ, PROJ), 1.0, 6.0, ((0, 16),))
    train_rows = normal_values(part_keys[1], (NT, PROJ), (9 * PROJ) ** -0.5, 0.015625, ((0, 16),))
    left_basis = normal_values(streams_of[2], (A_DIM, A_DIM), A_DIM ** -0.5, 0.5)
    right_basis = normal_values(streams_of[3], (B_DIM, B_DIM), B_DIM ** -0.5, 0.5)
    eigenvalues = jnp.clip(jnp.exp(jax.random.uniform(streams_of[4], (A_DIM, B_DIM), jnp.float32, math.log(0.01), math.log(10.0))), 0.01, 10.0)
    return dict(queries=queries, train_rows=train_rows, left_basis=left_basis, right_basis=right_basis, eigenvalues=eigenvalues)


DAMPING = 0.1


def precondition(row_block, left_basis, right_basis, eigenvalues):
    count = row_block.shape[0]
    highest = lax.Precision.HIGHEST
    matrix = row_block.reshape(count, A_DIM, B_DIM).astype(jnp.float32)
    left = left_basis.astype(jnp.float32)
    right = right_basis.astype(jnp.float32)
    inward = jnp.einsum("ai,qab->qib", left, matrix, precision=highest).astype(jnp.bfloat16)
    rotated = jnp.einsum("qib,bj->qij", inward.astype(jnp.float32), right, precision=highest)
    scaled = (rotated / (eigenvalues + DAMPING)).astype(jnp.bfloat16)
    restored = jnp.einsum("ai,qij->qaj", left, scaled.astype(jnp.float32), precision=highest).astype(jnp.bfloat16)
    prepared = jnp.einsum("qaj,bj->qab", restored.astype(jnp.float32), right, precision=highest).astype(jnp.bfloat16)
    return prepared.reshape(count, A_DIM * B_DIM)


def reference(queries, train_rows, left_basis, right_basis, eigenvalues):
    train_blocks = train_rows.reshape(NT // T_DEV, T_DEV, A_DIM * B_DIM)
    prepared = lax.map(lambda row_block: precondition(row_block, left_basis, right_basis, eigenvalues), train_blocks)
    prepared = prepared.reshape(NT, A_DIM * B_DIM)
    blocks = queries.reshape(NQ // Q_DEV, Q_DEV, A_DIM * B_DIM)

    def one_block(query_block):
        return lax.dot_general(query_block, prepared, (((1,), (1,)), ((), ())), preferred_element_type=jnp.float32)

    scores = lax.map(one_block, blocks)
    return scores.reshape(NQ, NT)
```

```python
import functools

import jax
import jax.numpy as jnp
import numpy as np
from jax import lax
from jax.experimental import pallas as pl
from jax.experimental.pallas import tpu as pltpu
from jax.sharding import PartitionSpec as P

A_DIM = 128
B_DIM = 128
LANES = 128
K_TILE = 2048

DAMPING = 0.1


def chip_ring(chips):
    if chips == 8:
        return list(range(0, chips, 2)) + list(range(chips - 1, 0, -2))
    return list(range(chips))


def precondition_kernel(rows_ref, left_ref, right_ref, eig_ref, out_ref, gather_ref, spread_ref):
    count = rows_ref.shape[0]
    for a in range(A_DIM):
        gather_ref[a * count:(a + 1) * count, :] = rows_ref[:, a * B_DIM:(a + 1) * B_DIM].astype(jnp.float32)
    left = left_ref[...]
    right = right_ref[...]
    damped = eig_ref[...] + DAMPING

    def stack(wide):
        return jnp.concatenate([wide[:, q * B_DIM:(q + 1) * B_DIM] for q in range(count)], axis=0)

    matrix = jnp.concatenate(
        [gather_ref[pl.ds(q, A_DIM, stride=count), :].astype(jnp.bfloat16) for q in range(count)], axis=1
    )
    inward = lax.dot_general(left, matrix, (((0,), (0,)), ((), ())), preferred_element_type=jnp.float32)
    rotated = jnp.dot(stack(inward.astype(jnp.bfloat16)), right, preferred_element_type=jnp.float32)
    scaled = jnp.concatenate(
        [(rotated[q * A_DIM:(q + 1) * A_DIM] / damped).astype(jnp.bfloat16) for q in range(count)], axis=1
    )
    restored = jnp.dot(left, scaled, preferred_element_type=jnp.float32).astype(jnp.bfloat16)
    prepared = lax.dot_general(
        stack(restored), right, (((1,), (1,)), ((), ())), preferred_element_type=jnp.float32
    )
    for q in range(count):
        spread_ref[pl.ds(q, A_DIM, stride=count), :] = prepared[q * A_DIM:(q + 1) * A_DIM]
    for a in range(A_DIM):
        out_ref[:, a * B_DIM:(a + 1) * B_DIM] = spread_ref[a * count:(a + 1) * count, :].astype(jnp.bfloat16)


def precondition(train_rows, left_basis, right_basis, eigenvalues, half):
    count = train_rows.shape[0] // 2
    width = train_rows.shape[1]
    whole = lambda shape: pl.BlockSpec(shape, lambda i: (0, 0))
    return pl.pallas_call(
        precondition_kernel,
        grid=(1,),
        out_shape=jax.ShapeDtypeStruct((count, width), jnp.bfloat16),
        in_specs=[pl.BlockSpec((count, width), lambda i: (half, 0))]
        + [whole(m.shape) for m in (left_basis, right_basis, eigenvalues)],
        out_specs=whole((count, width)),
        scratch_shapes=[pltpu.VMEM((A_DIM * count, B_DIM), jnp.float32)] * 2,
        compiler_params=pltpu.CompilerParams(vmem_limit_bytes=24 << 20),
        cost_estimate=pl.CostEstimate(
            flops=8 * count * A_DIM * A_DIM * B_DIM * 4, bytes_accessed=4 * count * width, transcendentals=0
        ),
        name="precondition",
    )(train_rows, left_basis, right_basis, eigenvalues)


def scores_kernel(slots, first, place_ref, query_ref, *refs):
    blocks = refs[:len(slots)]
    refs = refs[len(slots):]
    if not first:
        total_ref, refs = refs[0], refs[1:]
    out_ref, weight_ref, sum_ref = refs
    step = pl.program_id(0)
    count = blocks[0].shape[0]
    core = place_ref[2]

    @pl.when(step == 0)
    def _():
        weight_ref[...] = jnp.zeros_like(weight_ref)
        sum_ref[...] = jnp.zeros_like(sum_ref)

    per_block = LANES // (4 * count)
    for (group, other, half), block in zip(slots, blocks):
        owner = 1 - core if other else core
        start = group * LANES + lax.rem(place_ref[group], per_block) * 4 * count + owner * 2 * count + half * count
        weight_ref[pl.ds(pl.multiple_of(start, count), count), :] = block[...]
    sum_ref[...] += lax.dot_general(
        query_ref[...], weight_ref[...], (((1,), (1,)), ((), ())), preferred_element_type=jnp.float32
    )

    @pl.when(step == pl.num_programs(0) - 1)
    def _():
        out_ref[...] = jnp.zeros_like(out_ref) if first else total_ref[...]
        for group in range(weight_ref.shape[0] // LANES):
            start = lax.div(place_ref[group], per_block) * LANES
            lanes = pl.ds(pl.multiple_of(start, LANES), LANES)
            out_ref[:, lanes] += sum_ref[:, group * LANES:(group + 1) * LANES]


def add_scores(total, queries, place, slots, blocks, train_count):
    rows, width = queries.shape
    first = total is None
    groups = 1 + max(group for group, _, _ in slots)
    totals = [] if first else [total]
    whole = pl.BlockSpec((rows, train_count), lambda i: (0, 0))
    return pl.pallas_call(
        functools.partial(scores_kernel, slots, first),
        grid=(width // K_TILE,),
        out_shape=jax.ShapeDtypeStruct((rows, train_count), jnp.float32),
        in_specs=[pl.BlockSpec(memory_space=pltpu.SMEM), pl.BlockSpec((rows, K_TILE), lambda i: (0, i))]
        + [pl.BlockSpec((b.shape[0], K_TILE), lambda i: (0, i)) for b in blocks]
        + [whole] * len(totals),
        out_specs=whole,
        scratch_shapes=[
            pltpu.VMEM((groups * LANES, K_TILE), jnp.bfloat16),
            pltpu.VMEM((rows, groups * LANES), jnp.float32),
        ],
        compiler_params=pltpu.CompilerParams(vmem_limit_bytes=24 << 20),
        cost_estimate=pl.CostEstimate(
            flops=2 * rows * width * 256, bytes_accessed=2 * rows * width, transcendentals=0
        ),
        name="scores",
    )(place, queries, *blocks, *totals)


def per_device(queries, train_rows, left_basis, right_basis, eigenvalues):
    devices = lax.axis_size("wide")
    chips = devices // 2
    ring = chip_ring(chips)
    hops = chips // 2
    train_count = devices * train_rows.shape[0]

    def shift(step):
        return [
            (2 * ring[i] + core, 2 * ring[(i + step) % chips] + core) for i in range(chips) for core in range(2)
        ]

    swap = [(d, d ^ 1) for d in range(devices)]
    send = lambda block, pairs: lax.ppermute(block, "wide", pairs)
    up, down = shift(1), shift(-1)

    table = np.zeros((devices, hops + 1, 4), np.int32)
    for i in range(chips):
        for core in range(2):
            for hop in range(hops + 1):
                table[2 * ring[i] + core, hop] = (ring[(i - hop) % chips], ring[(i + hop) % chips], core, 0)
    places = lax.dynamic_index_in_dim(jnp.asarray(table), lax.axis_index("wide"), 0, keepdims=False)

    own = [precondition(train_rows, left_basis, right_basis, eigenvalues, half) for half in range(2)]
    others = [send(block, swap) for block in own]
    total = add_scores(
        None, queries, places[0], [(0, 0, 0), (0, 0, 1), (0, 1, 0), (0, 1, 1)], own + others, train_count
    )
    rising, falling = list(own), list(own)
    for hop in range(1, hops + 1):
        slots, blocks = [], []
        last = hop == hops
        for half in range(2):
            if not last or half == 0:
                rising[half] = send(rising[half], up)
                blocks += [rising[half], send(rising[half], swap)]
                slots += [(0, 0, half), (0, 1, half)]
            if not last or half == 1:
                falling[half] = send(falling[half], down)
                blocks += [falling[half], send(falling[half], swap)]
                group = 0 if last else 1
                slots += [(group, 0, half), (group, 1, half)]
        total = add_scores(total, queries, places[hop], slots, blocks, train_count)
    return total


def solution(mesh):
    in_specs = (P(("grp", "wide"), None), P(("grp", "wide"), None), P(), P(), P())
    out_specs = P(("grp", "wide"), None)
    return jax.shard_map(
        per_device, mesh=mesh, in_specs=in_specs, out_specs=out_specs, check_vma=False
    )
```

```python
import functools

import jax
import jax.numpy as jnp
import numpy as np
from jax import lax
from jax.experimental import pallas as pl
from jax.experimental.pallas import tpu as pltpu
from jax.sharding import PartitionSpec as P

A_DIM = 128
B_DIM = 128
LANES = 128
K_TILE = 4096
KERNEL_VMEM = 16 << 20
PREPARE_COST = pl.CostEstimate(flops=1, bytes_accessed=1, transcendentals=0)
SCORE_COST = pl.CostEstimate(flops=1, bytes_accessed=1, transcendentals=0)
ANY_SPEC = pl.BlockSpec(memory_space=pl.ANY)
VMEM_SPEC = pl.BlockSpec(memory_space=pltpu.VMEM)

DAMPING = 0.1


def chip_ring(chips):
    if chips == 8:
        return list(range(0, chips, 2)) + list(range(chips - 1, 0, -2))
    return list(range(chips))


def precondition_kernel(*refs):
    sources, out_ref, arrived = refs[:4], refs[4], refs[5:9]
    gather_ref, spread_ref, sems = refs[9:]
    fetches = [pltpu.make_async_copy(a, b, sems.at[i]) for i, (a, b) in enumerate(zip(sources, arrived))]
    for fetch in fetches:
        fetch.start()
    for fetch in fetches:
        fetch.wait()
    rows_ref, left_ref, right_ref, eig_ref = arrived
    count = gather_ref.shape[0] // A_DIM
    left = left_ref[...]
    right = right_ref[...]
    damped = eig_ref[...] + DAMPING

    def stack(wide):
        return jnp.concatenate([wide[:, q * B_DIM:(q + 1) * B_DIM] for q in range(count)], axis=0)

    for base in range(0, rows_ref.shape[0], count):
        rows = slice(base, base + count)
        for a in range(A_DIM):
            gather_ref[a * count:(a + 1) * count, :] = rows_ref[rows, a * B_DIM:(a + 1) * B_DIM].astype(jnp.float32)
        matrix = jnp.concatenate(
            [gather_ref[pl.ds(q, A_DIM, stride=count), :].astype(jnp.bfloat16) for q in range(count)], axis=1
        )
        inward = lax.dot_general(left, matrix, (((0,), (0,)), ((), ())), preferred_element_type=jnp.float32)
        rotated = jnp.dot(stack(inward.astype(jnp.bfloat16)), right, preferred_element_type=jnp.float32)
        scaled = jnp.concatenate(
            [(rotated[q * A_DIM:(q + 1) * A_DIM] / damped).astype(jnp.bfloat16) for q in range(count)], axis=1
        )
        restored = jnp.dot(left, scaled, preferred_element_type=jnp.float32).astype(jnp.bfloat16)
        prepared = lax.dot_general(
            stack(restored), right, (((1,), (1,)), ((), ())), preferred_element_type=jnp.float32
        )
        for q in range(count):
            spread_ref[pl.ds(q, A_DIM, stride=count), :] = prepared[q * A_DIM:(q + 1) * A_DIM]
        for a in range(A_DIM):
            out_ref[rows, a * B_DIM:(a + 1) * B_DIM] = spread_ref[a * count:(a + 1) * count, :].astype(jnp.bfloat16)


def precondition(rows, *factors):
    operands = rows, *[pltpu.with_memory_space_constraint(m, pltpu.HBM) for m in factors]
    return pl.pallas_call(
        precondition_kernel,
        out_shape=jax.ShapeDtypeStruct(rows.shape, jnp.bfloat16),
        in_specs=[ANY_SPEC] * 4,
        out_specs=VMEM_SPEC,
        scratch_shapes=[pltpu.VMEM(m.shape, m.dtype) for m in operands]
        + [pltpu.VMEM((A_DIM * 16, B_DIM), jnp.float32)] * 2
        + [pltpu.SemaphoreType.DMA((4,))],
        compiler_params=pltpu.CompilerParams(vmem_limit_bytes=KERNEL_VMEM),
        cost_estimate=PREPARE_COST,
        name="precondition",
    )(*operands)


def scores_kernel(entries, first, last, owners_ref, query_ref, *refs):
    blocks, refs = refs[:len(entries)], refs[len(entries):]
    if not first:
        total_ref, refs = refs[0], refs[1:]
    out_ref, weight_ref, sum_ref, sems = refs
    height, width = blocks[0].shape
    steps = width // K_TILE

    def fetches(step):
        return [
            pltpu.make_async_copy(
                block.at[:, pl.ds(pl.multiple_of(step * K_TILE, K_TILE), K_TILE)],
                weight_ref.at[lax.rem(step, 2), pl.ds(i * height, height), :],
                sems.at[lax.rem(step, 2), i],
            )
            for i, block in enumerate(blocks)
        ]

    for fetch in fetches(0):
        fetch.start()
    if first:
        out_ref[...] = jnp.zeros_like(out_ref)
    if last:
        out_ref[...] = total_ref[...]
    sum_ref[...] = jnp.zeros_like(sum_ref)

    @pl.loop(0, steps)
    def _(step):
        @pl.when(step + 1 < steps)
        def _():
            for fetch in fetches(step + 1):
                fetch.start()

        for fetch in fetches(step):
            fetch.wait()
        sum_ref[...] += lax.dot_general(
            query_ref[:, pl.ds(pl.multiple_of(step * K_TILE, K_TILE), K_TILE)],
            weight_ref[lax.rem(step, 2)],
            (((1,), (1,)), ((), ())),
            preferred_element_type=jnp.float32,
        )

    place = lax.broadcasted_iota(jnp.int32, sum_ref.shape, 1) // height
    per_tile = LANES // height
    for i, entry in enumerate(entries):
        owner = owners_ref[entry]
        spot = lax.rem(owner, per_tile)
        moved = pltpu.roll(sum_ref[...], lax.rem(spot - i + per_tile, per_tile) * height, 1)
        lanes = pl.ds(pl.multiple_of(lax.div(owner, per_tile) * LANES, LANES), LANES)
        out_ref[:, lanes] += jnp.where(place == spot, moved, 0.0)


def add_scores(total, queries, owners, entries, blocks, train_count, last):
    rows = queries.shape[0]
    first = total is None
    operands = [pltpu.with_memory_space_constraint(queries, pltpu.VMEM), *blocks] + ([] if first else [total])
    return pl.pallas_call(
        functools.partial(scores_kernel, entries, first, last),
        out_shape=jax.ShapeDtypeStruct((rows, train_count), jnp.float32),
        in_specs=[pl.BlockSpec(memory_space=pltpu.SMEM), VMEM_SPEC]
        + [ANY_SPEC] * len(blocks)
        + ([] if first else [VMEM_SPEC]),
        out_specs=VMEM_SPEC,
        scratch_shapes=[
            pltpu.VMEM((2, LANES, K_TILE), jnp.bfloat16),
            pltpu.VMEM((rows, LANES), jnp.float32),
            pltpu.SemaphoreType.DMA((2, len(blocks))),
        ],
        input_output_aliases={} if first or last else {len(operands): 0},
        compiler_params=pltpu.CompilerParams(vmem_limit_bytes=KERNEL_VMEM),
        cost_estimate=SCORE_COST,
        name="scores",
    )(owners, *operands)


def per_device(queries, train_rows, left_basis, right_basis, eigenvalues):
    devices = lax.axis_size("wide")
    chips = devices // 2
    ring = chip_ring(chips)
    hops = chips // 2
    train_count = devices * train_rows.shape[0]

    along = [
        (2 * ring[i] + core, 2 * ring[(i + (-1 if core else 1)) % chips] + core)
        for i in range(chips)
        for core in range(2)
    ]
    across = [(d, d ^ 1) for d in range(devices)]
    send = lambda block, pairs: lax.ppermute(block, "wide", pairs)

    table = np.zeros((devices, devices), np.int32)
    for i in range(chips):
        for core in range(2):
            row = [2 * ring[i] + core, 2 * ring[i] + 1 - core]
            for arrival in range(1, chips):
                hop, swapped = (arrival + 1) // 2, (arrival + 1) % 2
                step = hop if core else -hop
                row += [
                    2 * ring[(i + step) % chips] + (core ^ swapped),
                    2 * ring[(i - step) % chips] + (1 ^ core ^ swapped),
                ]
            table[row[0]] = row
    owners = lax.dynamic_index_in_dim(jnp.asarray(table), lax.axis_index("wide"), 0, keepdims=False)

    def after(block, array):
        return lax.optimization_barrier((block, array))

    raw = train_rows
    factors = left_basis, right_basis, eigenvalues
    other = precondition(send(train_rows, across), *factors)
    train_rows, other = after(train_rows, other)
    own = precondition(train_rows, *factors)
    chains = [raw, other]
    blocks = [own, other]
    total, done = None, 0
    for arrival in range(1, chips):
        chain = (arrival + 1) % 2
        block = send(chains[chain], along)
        if arrival > 2 and chain == 0:
            entries = list(range(done, done + 4))
            total = add_scores(total, queries, owners, entries, [blocks[e] for e in entries], train_count, False)
            done += 4
            block, total = after(block, total)
        if arrival == 1:
            block = precondition(block, *factors)
        if arrival > 1 and chain == 1:
            if total is None:
                own, block = after(own, block)
                blocks[0] = own
            else:
                total, block = after(total, block)
        chains[chain] = block
        blocks += [block, send(block, across)]
    return add_scores(total, queries, owners, list(range(done, devices)), blocks[done:], train_count, True)


def solution(mesh):
    in_specs = (P(("grp", "wide"), None), P(("grp", "wide"), None), P(), P(), P())
    out_specs = P(("grp", "wide"), None)
    return jax.shard_map(
        per_device, mesh=mesh, in_specs=in_specs, out_specs=out_specs, check_vma=False
    )
```

```python
import functools

import jax
import jax.numpy as jnp
import numpy as np
from jax import lax
from jax.experimental import pallas as pl
from jax.experimental.pallas import tpu as pltpu
from jax.sharding import PartitionSpec as P

A_DIM = 128
B_DIM = 128
LANES = 128
K_TILE = 4608
KERNEL_VMEM = 16 << 20
PREPARE_COST = pl.CostEstimate(flops=1, bytes_accessed=1, transcendentals=0)
SCORE_COST = pl.CostEstimate(flops=1, bytes_accessed=1, transcendentals=0)
CUT_COST = pl.CostEstimate(flops=1, bytes_accessed=1, transcendentals=0)
LAST_PARTS = 7, 9
ANY_SPEC = pl.BlockSpec(memory_space=pl.ANY)
VMEM_SPEC = pl.BlockSpec(memory_space=pltpu.VMEM)

DAMPING = 0.1


def chip_ring(chips):
    if chips == 8:
        return list(range(0, chips, 2)) + list(range(chips - 1, 0, -2))
    return list(range(chips))


def precondition_kernel(*refs):
    sources, out_ref, arrived = refs[:4], refs[4], refs[5:9]
    gather_ref, spread_ref, sems = refs[9:]
    fetches = [pltpu.make_async_copy(a, b, sems.at[i]) for i, (a, b) in enumerate(zip(sources, arrived))]
    for fetch in fetches:
        fetch.start()
    for fetch in fetches:
        fetch.wait()
    rows_ref, left_ref, right_ref, eig_ref = arrived
    count = gather_ref.shape[0] // A_DIM
    left = left_ref[...]
    right = right_ref[...]
    damped = eig_ref[...] + DAMPING

    def stack(wide):
        return jnp.concatenate([wide[:, q * B_DIM:(q + 1) * B_DIM] for q in range(count)], axis=0)

    for base in range(0, rows_ref.shape[0], count):
        rows = slice(base, base + count)
        for a in range(A_DIM):
            gather_ref[a * count:(a + 1) * count, :] = rows_ref[rows, a * B_DIM:(a + 1) * B_DIM].astype(jnp.float32)
        matrix = jnp.concatenate(
            [gather_ref[pl.ds(q, A_DIM, stride=count), :].astype(jnp.bfloat16) for q in range(count)], axis=1
        )
        inward = lax.dot_general(left, matrix, (((0,), (0,)), ((), ())), preferred_element_type=jnp.float32)
        rotated = jnp.dot(stack(inward.astype(jnp.bfloat16)), right, preferred_element_type=jnp.float32)
        scaled = jnp.concatenate(
            [(rotated[q * A_DIM:(q + 1) * A_DIM] / damped).astype(jnp.bfloat16) for q in range(count)], axis=1
        )
        restored = jnp.dot(left, scaled, preferred_element_type=jnp.float32).astype(jnp.bfloat16)
        prepared = lax.dot_general(
            stack(restored), right, (((1,), (1,)), ((), ())), preferred_element_type=jnp.float32
        )
        for q in range(count):
            spread_ref[pl.ds(q, A_DIM, stride=count), :] = prepared[q * A_DIM:(q + 1) * A_DIM]
        for a in range(A_DIM):
            out_ref[rows, a * B_DIM:(a + 1) * B_DIM] = spread_ref[a * count:(a + 1) * count, :].astype(jnp.bfloat16)


def precondition(rows, *factors):
    operands = rows, *[pltpu.with_memory_space_constraint(m, pltpu.HBM) for m in factors]
    return pl.pallas_call(
        precondition_kernel,
        out_shape=jax.ShapeDtypeStruct(rows.shape, jnp.bfloat16),
        in_specs=[ANY_SPEC] * 4,
        out_specs=VMEM_SPEC,
        scratch_shapes=[pltpu.VMEM(m.shape, m.dtype) for m in operands]
        + [pltpu.VMEM((A_DIM * 16, B_DIM), jnp.float32)] * 2
        + [pltpu.SemaphoreType.DMA((4,))],
        compiler_params=pltpu.CompilerParams(vmem_limit_bytes=KERNEL_VMEM),
        cost_estimate=PREPARE_COST,
        name="precondition",
    )(*operands)


def scores_kernel(entries, count, begin, first, last, owners_ref, query_ref, *refs):
    blocks, refs = refs[:count], refs[count:]
    if not first:
        total_ref, refs = refs[0], refs[1:]
    out_ref, sum_ref = refs
    height = blocks[0].shape[0]
    width = min(block.shape[1] for block in blocks)
    tile = column_tile(width)
    missing = sum_ref.shape[1] - sum(block.shape[0] for block in blocks)
    if first:
        out_ref[...] = jnp.zeros_like(out_ref)
    if last:
        out_ref[...] = total_ref[...]
    sum_ref[...] = jnp.zeros_like(sum_ref)

    @pl.loop(0, width // tile)
    def _(step):
        def columns(skipped):
            return pl.ds(pl.multiple_of(skipped + step * tile, LANES), tile)

        rows = [block[:, columns(begin if block.shape[1] > width else 0)] for block in blocks]
        if missing:
            rows.append(jnp.zeros((missing, tile), rows[0].dtype))
        sum_ref[...] += lax.dot_general(
            query_ref[:, columns(begin)], jnp.concatenate(rows, axis=0), (((1,), (1,)), ((), ())),
            preferred_element_type=jnp.float32,
        )

    per_tile = LANES // height
    place = lax.broadcasted_iota(jnp.int32, (sum_ref.shape[0], LANES), 1) // height
    for i, entry in enumerate(entries):
        owner = owners_ref[entry]
        spot = lax.rem(owner, per_tile)
        held = sum_ref[:, i // per_tile * LANES:(i // per_tile + 1) * LANES]
        moved = pltpu.roll(held, lax.rem(spot - i % per_tile + per_tile, per_tile) * height, 1)
        lanes = pl.ds(pl.multiple_of(lax.div(owner, per_tile) * LANES, LANES), LANES)
        out_ref[:, lanes] += jnp.where(place == spot, moved, 0.0)


def column_tile(width):
    return max(t for t in range(LANES, min(K_TILE, width) + 1, LANES) if width % t == 0)


def add_scores(total, queries, owners, entries, blocks, train_count, begin=0, last=False):
    rows = queries.shape[0]
    first = total is None
    operands = [pltpu.with_memory_space_constraint(queries, pltpu.VMEM), *blocks] + ([] if first else [total])
    lanes = -(-len(entries) * blocks[0].shape[0] // LANES) * LANES
    return pl.pallas_call(
        functools.partial(scores_kernel, entries, len(blocks), begin, first, last),
        out_shape=jax.ShapeDtypeStruct((rows, train_count), jnp.float32),
        in_specs=[pl.BlockSpec(memory_space=pltpu.SMEM)] + [VMEM_SPEC] * len(operands),
        out_specs=VMEM_SPEC,
        scratch_shapes=[pltpu.VMEM((rows, lanes), jnp.float32)],
        input_output_aliases={} if first or last else {len(operands): 0},
        compiler_params=pltpu.CompilerParams(vmem_limit_bytes=KERNEL_VMEM),
        cost_estimate=SCORE_COST,
        name="scores",
    )(owners, *operands)


def cut_kernel(source_ref, *pieces):
    row, column = 0, 0
    for piece in pieces:
        height, width = piece.shape
        piece[...] = source_ref[row:row + height, column:column + width]
        row, column = (row + height) % source_ref.shape[0], (column + width) % source_ref.shape[1]


def cut(block, shapes):
    return pl.pallas_call(
        cut_kernel,
        out_shape=[jax.ShapeDtypeStruct(shape, block.dtype) for shape in shapes],
        in_specs=[VMEM_SPEC],
        out_specs=[VMEM_SPEC] * len(shapes),
        compiler_params=pltpu.CompilerParams(vmem_limit_bytes=KERNEL_VMEM),
        cost_estimate=CUT_COST,
        name="cut",
    )(block)


def per_device(queries, train_rows, left_basis, right_basis, eigenvalues):
    devices = lax.axis_size("wide")
    chips = devices // 2
    ring = chip_ring(chips)
    hops = chips // 2
    train_count = devices * train_rows.shape[0]
    height, width = train_rows.shape

    along = [
        (2 * ring[i] + core, 2 * ring[(i + (-1 if core else 1)) % chips] + core)
        for i in range(chips)
        for core in range(2)
    ]
    across = [(d, d ^ 1) for d in range(devices)]
    send = lambda block, pairs: lax.ppermute(block, "wide", pairs)

    table = np.zeros((devices, devices), np.int32)
    for i in range(chips):
        for core in range(2):
            row = [2 * ring[i] + core, 2 * ring[i] + 1 - core]
            for arrival in range(1, chips):
                hop, swapped = (arrival + 1) // 2, (arrival + 1) % 2
                step = hop if core else -hop
                row += [
                    2 * ring[(i + step) % chips] + (core ^ swapped),
                    2 * ring[(i - step) % chips] + (1 ^ core ^ swapped),
                ]
            table[row[0]] = row
    owners = lax.dynamic_index_in_dim(jnp.asarray(table), lax.axis_index("wide"), 0, keepdims=False)

    def after(block, array):
        return lax.optimization_barrier((block, array))

    raw = train_rows
    factors = left_basis, right_basis, eigenvalues
    other = precondition(send(train_rows, across), *factors)
    train_rows, other = after(train_rows, other)
    own = precondition(train_rows, *factors)
    chains = [raw, other]
    blocks = [own, other]
    score = lambda total, arrivals, blocks, **kw: add_scores(
        total, queries, owners, [e for a in arrivals for e in (2 * a, 2 * a + 1)], blocks, train_count, **kw
    )
    pairs = [[own, other]]
    groups = [[a, a + 1] for a in range(0, chips - 6, 2)] + [[chips - 6, chips - 5, chips - 4]]
    total = None
    for arrival in range(1, chips - 1):
        chain = (arrival + 1) % 2
        block = send(chains[chain], along)
        if groups[0][-1] == arrival - 2:
            total = score(total, groups[0], [block for a in groups[0] for block in pairs[a]])
            groups.pop(0)
            block, total = after(block, total)
        if arrival == 1:
            block = precondition(block, *factors)
        if groups and groups[0][-1] == arrival - 1:
            if total is None:
                pairs[0][0], block = after(pairs[0][0], block)
            else:
                total, block = after(total, block)
        chains[chain] = block
        halves = cut(block, [(height // 2, width)] * 2) if arrival == chips - 2 else [block]
        pairs.append([block] + [send(half, across) for half in halves])

    group = [chips - 3, chips - 2, chips - 1]
    widths = [width * part // sum(LAST_PARTS) for part in LAST_PARTS]
    begin = 0
    for i, piece in enumerate(cut(chains[0], [(height, w) for w in widths])):
        if i == 1:
            piece, block = after(piece, block)
            pairs[-2 if len(pairs) == chips else -1][0] = block
        last = i == len(widths) - 1
        part = send(piece, along)
        if i:
            total = score(total, group, blocks, begin=begin)
            begin += widths[i - 1]
            part, total = after(part, total)
        swapped = [part] if last else cut(part, [(height // 2, widths[i])] * 2)
        blocks = pairs[chips - 3] + pairs[chips - 2] + [part] + [send(piece, across) for piece in swapped]
    return score(total, group, blocks, begin=begin, last=True)


def solution(mesh):
    in_specs = (P(("grp", "wide"), None), P(("grp", "wide"), None), P(), P(), P())
    out_specs = P(("grp", "wide"), None)
    return jax.shard_map(
        per_device, mesh=mesh, in_specs=in_specs, out_specs=out_specs, check_vma=False
    )
```

```python
import functools

import jax
import jax.numpy as jnp
from jax import lax
from jax.experimental import pallas as pl
from jax.experimental.pallas import tpu as pltpu
from jax.sharding import PartitionSpec as P

A_DIM = 128
B_DIM = 128
LANES = 128
K_TILE = 9216
RESULT_PARTS = 4
KERNEL_VMEM = 16 << 20
PREPARE_COST = pl.CostEstimate(flops=1, bytes_accessed=1, transcendentals=0)
SCORE_COST = pl.CostEstimate(flops=1, bytes_accessed=1, transcendentals=0)
CUT_COST = pl.CostEstimate(flops=1, bytes_accessed=1, transcendentals=0)
LAST_PARTS = 15, 17
ANY_SPEC = pl.BlockSpec(memory_space=pl.ANY)
VMEM_SPEC = pl.BlockSpec(memory_space=pltpu.VMEM)

DAMPING = 0.1


def chip_ring(chips):
    if chips == 8:
        return list(range(0, chips, 2)) + list(range(chips - 1, 0, -2))
    return list(range(chips))


def precondition_kernel(*refs):
    sources, out_ref, arrived = refs[:4], refs[4], refs[5:9]
    gather_ref, spread_ref, sems = refs[9:]
    fetches = [pltpu.make_async_copy(a, b, sems.at[i]) for i, (a, b) in enumerate(zip(sources, arrived))]
    for fetch in fetches:
        fetch.start()
    for fetch in fetches:
        fetch.wait()
    rows_ref, left_ref, right_ref, eig_ref = arrived
    count = gather_ref.shape[0] // A_DIM
    left = left_ref[...]
    right = right_ref[...]
    damped = eig_ref[...] + DAMPING

    def stack(wide):
        return jnp.concatenate([wide[:, q * B_DIM:(q + 1) * B_DIM] for q in range(count)], axis=0)

    for base in range(0, rows_ref.shape[0], count):
        rows = slice(base, base + count)
        for a in range(A_DIM):
            gather_ref[a * count:(a + 1) * count, :] = rows_ref[rows, a * B_DIM:(a + 1) * B_DIM].astype(jnp.float32)
        matrix = jnp.concatenate(
            [gather_ref[pl.ds(q, A_DIM, stride=count), :].astype(jnp.bfloat16) for q in range(count)], axis=1
        )
        inward = lax.dot_general(left, matrix, (((0,), (0,)), ((), ())), preferred_element_type=jnp.float32)
        rotated = jnp.dot(stack(inward.astype(jnp.bfloat16)), right, preferred_element_type=jnp.float32)
        scaled = jnp.concatenate(
            [(rotated[q * A_DIM:(q + 1) * A_DIM] / damped).astype(jnp.bfloat16) for q in range(count)], axis=1
        )
        restored = jnp.dot(left, scaled, preferred_element_type=jnp.float32).astype(jnp.bfloat16)
        prepared = lax.dot_general(
            stack(restored), right, (((1,), (1,)), ((), ())), preferred_element_type=jnp.float32
        )
        for q in range(count):
            spread_ref[pl.ds(q, A_DIM, stride=count), :] = prepared[q * A_DIM:(q + 1) * A_DIM]
        for a in range(A_DIM):
            out_ref[rows, a * B_DIM:(a + 1) * B_DIM] = spread_ref[a * count:(a + 1) * count, :].astype(jnp.bfloat16)


def precondition(rows, *factors):
    operands = rows, *[pltpu.with_memory_space_constraint(m, pltpu.HBM) for m in factors]
    return pl.pallas_call(
        precondition_kernel,
        out_shape=jax.ShapeDtypeStruct(rows.shape, jnp.bfloat16),
        in_specs=[ANY_SPEC] * 4,
        out_specs=VMEM_SPEC,
        scratch_shapes=[pltpu.VMEM(m.shape, m.dtype) for m in operands]
        + [pltpu.VMEM((A_DIM * 16, B_DIM), jnp.float32)] * 2
        + [pltpu.SemaphoreType.DMA((4,))],
        compiler_params=pltpu.CompilerParams(vmem_limit_bytes=KERNEL_VMEM),
        cost_estimate=PREPARE_COST,
        name="precondition",
    )(*operands)


def owner_of(entry, chips):
    here = lax.axis_index("wide")
    arrival, side = entry // 2, entry % 2
    chip, core = lax.div(here, 2), lax.rem(here, 2)
    hop, crossed = (arrival + 1) // 2, (arrival + 1) % 2 if arrival else 0
    step = jnp.where(core == side, -hop, hop)
    ladder = chips == 8
    spot = jnp.where(lax.rem(chip, 2) == 0, lax.div(chip, 2), chips - 1 - lax.div(chip, 2)) if ladder else chip
    spot = lax.rem(spot + step + chips, chips)
    chip = jnp.where(spot < chips // 2, 2 * spot, 2 * chips - 1 - 2 * spot) if ladder else spot
    return 2 * chip + (1 - core if (side + crossed) % 2 else core)


def scores_kernel(entries, count, begin, first, last, query_ref, *refs):
    blocks, refs = refs[:count], refs[count:]
    if not first:
        total_ref, refs = refs[0], refs[1:]
    out_ref, sum_ref = refs[:2]
    height = blocks[0].shape[0]
    width = min(block.shape[1] for block in blocks)
    tile = column_tile(width)
    steps = width // tile
    missing = sum_ref.shape[1] - sum(block.shape[0] for block in blocks)
    chips = out_ref.shape[1] // height // 2
    if first:
        out_ref[...] = jnp.zeros_like(out_ref)

    def product(step):
        def columns(skipped):
            return pl.ds(pl.multiple_of(skipped + step * tile, LANES), tile)

        rows = [block[:, columns(begin if block.shape[1] > width else 0)] for block in blocks]
        if missing:
            rows.append(jnp.zeros((missing, tile), rows[0].dtype))
        return lax.dot_general(
            query_ref[:, columns(begin)], jnp.concatenate(rows, axis=0), (((1,), (1,)), ((), ())),
            preferred_element_type=jnp.float32,
        )

    sum_ref[...] = product(0)
    if steps > 1:
        @pl.loop(1, steps)
        def _(step):
            sum_ref[...] += product(step)

    per_tile = LANES // height
    owners = [owner_of(entry, chips) for entry in entries]

    def add(target_ref, rows):
        place = lax.broadcasted_iota(jnp.int32, (rows.size, LANES), 1) // height
        for i, owner in enumerate(owners):
            spot = lax.rem(owner, per_tile)
            held = sum_ref[rows, i // per_tile * LANES:(i // per_tile + 1) * LANES]
            moved = pltpu.roll(held, lax.rem(spot - i % per_tile + per_tile, per_tile) * height, 1)
            lanes = pl.ds(pl.multiple_of(lax.div(owner, per_tile) * LANES, LANES), LANES)
            target_ref[rows, lanes] += jnp.where(place == spot, moved, 0.0)

    if not last:
        add(out_ref, pl.ds(0, out_ref.shape[0]))
        return
    result_ref, sems = refs[2:]
    size = out_ref.shape[0] // RESULT_PARTS
    copies = []
    for i in range(RESULT_PARTS):
        rows = pl.ds(i * size, size)
        result_ref[rows, :] = total_ref[rows, :]
        add(result_ref, rows)
        copies.append(pltpu.make_async_copy(result_ref.at[rows, :], out_ref.at[rows, :], sems.at[i]))
        copies[-1].start()
    for copy in copies:
        copy.wait()


def column_tile(width):
    return max(t for t in range(LANES, min(K_TILE, width) + 1, LANES) if width % t == 0)


def add_scores(total, queries, entries, blocks, train_count, begin=0, last=False):
    rows = queries.shape[0]
    first = total is None
    operands = [pltpu.with_memory_space_constraint(queries, pltpu.VMEM), *blocks] + ([] if first else [total])
    lanes = -(-len(entries) * blocks[0].shape[0] // LANES) * LANES
    result = [pltpu.VMEM((rows, train_count), jnp.float32), pltpu.SemaphoreType.DMA((RESULT_PARTS,))]
    return pl.pallas_call(
        functools.partial(scores_kernel, entries, len(blocks), begin, first, last),
        out_shape=jax.ShapeDtypeStruct((rows, train_count), jnp.float32),
        in_specs=[VMEM_SPEC] * len(operands),
        out_specs=ANY_SPEC if last else VMEM_SPEC,
        scratch_shapes=[pltpu.VMEM((rows, lanes), jnp.float32)] + (result if last else []),
        input_output_aliases={} if first or last else {len(operands) - 1: 0},
        compiler_params=pltpu.CompilerParams(vmem_limit_bytes=KERNEL_VMEM),
        cost_estimate=SCORE_COST,
        name="scores",
    )(*operands)


def cut_kernel(source_ref, *pieces):
    row, column = 0, 0
    for piece in pieces:
        height, width = piece.shape
        piece[...] = source_ref[row:row + height, column:column + width]
        row, column = (row + height) % source_ref.shape[0], (column + width) % source_ref.shape[1]


def cut(block, shapes):
    return pl.pallas_call(
        cut_kernel,
        out_shape=[jax.ShapeDtypeStruct(shape, block.dtype) for shape in shapes],
        in_specs=[VMEM_SPEC],
        out_specs=[VMEM_SPEC] * len(shapes),
        compiler_params=pltpu.CompilerParams(vmem_limit_bytes=KERNEL_VMEM),
        cost_estimate=CUT_COST,
        name="cut",
    )(block)


def per_device(queries, train_rows, left_basis, right_basis, eigenvalues):
    devices = lax.axis_size("wide")
    chips = devices // 2
    ring = chip_ring(chips)
    hops = chips // 2
    train_count = devices * train_rows.shape[0]
    height, width = train_rows.shape

    along = [
        (2 * ring[i] + core, 2 * ring[(i + (-1 if core else 1)) % chips] + core)
        for i in range(chips)
        for core in range(2)
    ]
    across = [(d, d ^ 1) for d in range(devices)]
    send = lambda block, pairs: lax.ppermute(block, "wide", pairs)

    def after(block, array):
        return lax.optimization_barrier((block, array))

    raw = train_rows
    factors = left_basis, right_basis, eigenvalues
    other = precondition(send(train_rows, across), *factors)
    train_rows, other = after(train_rows, other)
    own = precondition(train_rows, *factors)
    chains = [raw, other]
    blocks = [own, other]
    score = lambda total, arrivals, blocks, **kw: add_scores(
        total, queries, [e for a in arrivals for e in (2 * a, 2 * a + 1)], blocks, train_count, **kw
    )
    pairs = [[own, other]]
    groups = [[a, a + 1] for a in range(0, chips - 6, 2)] + [[chips - 6, chips - 5, chips - 4]]
    total = None
    for arrival in range(1, chips - 1):
        chain = (arrival + 1) % 2
        block = send(chains[chain], along)
        if groups[0][-1] == arrival - 2:
            total = score(total, groups[0], [block for a in groups[0] for block in pairs[a]])
            groups.pop(0)
            block, total = after(block, total)
        if arrival == 1:
            block = precondition(block, *factors)
        if groups and groups[0][-1] == arrival - 1:
            if total is None:
                pairs[0][0], block = after(pairs[0][0], block)
            else:
                total, block = after(total, block)
        chains[chain] = block
        halves = cut(block, [(height // 2, width)] * 2) if arrival == chips - 2 else [block]
        pairs.append([block] + [send(half, across) for half in halves])

    group = [chips - 3, chips - 2, chips - 1]
    widths = [width * part // sum(LAST_PARTS) for part in LAST_PARTS]
    begin = 0
    for i, piece in enumerate(cut(chains[0], [(height, w) for w in widths])):
        if i == 1:
            piece, block = after(piece, block)
            pairs[-2 if len(pairs) == chips else -1][0] = block
        last = i == len(widths) - 1
        part = send(piece, along)
        if i:
            total = score(total, group, blocks, begin=begin)
            begin += widths[i - 1]
            part, total = after(part, total)
        swapped = [part]
        blocks = pairs[chips - 3] + pairs[chips - 2] + [part] + [send(piece, across) for piece in swapped]
    return score(total, group, blocks, begin=begin, last=True)


def solution(mesh):
    in_specs = (P(("grp", "wide"), None), P(("grp", "wide"), None), P(), P(), P())
    out_specs = P(("grp", "wide"), None)
    return jax.shard_map(
        per_device, mesh=mesh, in_specs=in_specs, out_specs=out_specs, check_vma=False
    )
```

```python
import functools

import jax
import jax.numpy as jnp
from jax import lax
from jax.experimental import pallas as pl
from jax.experimental.pallas import tpu as pltpu
from jax.sharding import PartitionSpec as P

A_DIM = 128
B_DIM = 128
LANES = 128
K_TILE = 9216
RESULT_PARTS = 4
KERNEL_VMEM = 16 << 20
PREPARE_COST = pl.CostEstimate(flops=1, bytes_accessed=1, transcendentals=0)
SCORE_COST = pl.CostEstimate(flops=1, bytes_accessed=1, transcendentals=0)
CUT_COST = pl.CostEstimate(flops=1, bytes_accessed=1, transcendentals=0)
LAST_PARTS = 17, 15
ANY_SPEC = pl.BlockSpec(memory_space=pl.ANY)
VMEM_SPEC = pl.BlockSpec(memory_space=pltpu.VMEM)

DAMPING = 0.1


def chip_ring(chips):
    if chips == 8:
        return list(range(0, chips, 2)) + list(range(chips - 1, 0, -2))
    return list(range(chips))


def precondition_kernel(*refs):
    sources, out_ref, arrived = refs[:4], refs[4], refs[5:9]
    gather_ref, spread_ref, sems = refs[9:]
    fetches = [pltpu.make_async_copy(a, b, sems.at[i]) for i, (a, b) in enumerate(zip(sources, arrived))]
    for fetch in fetches:
        fetch.start()
    for fetch in fetches:
        fetch.wait()
    rows_ref, left_ref, right_ref, eig_ref = arrived
    count = gather_ref.shape[0] // A_DIM
    left = left_ref[...]
    right = right_ref[...]
    damped = eig_ref[...] + DAMPING

    def stack(wide):
        return jnp.concatenate([wide[:, q * B_DIM:(q + 1) * B_DIM] for q in range(count)], axis=0)

    for base in range(0, rows_ref.shape[0], count):
        rows = slice(base, base + count)
        for a in range(A_DIM):
            gather_ref[a * count:(a + 1) * count, :] = rows_ref[rows, a * B_DIM:(a + 1) * B_DIM].astype(jnp.float32)
        matrix = jnp.concatenate(
            [gather_ref[pl.ds(q, A_DIM, stride=count), :].astype(jnp.bfloat16) for q in range(count)], axis=1
        )
        inward = lax.dot_general(left, matrix, (((0,), (0,)), ((), ())), preferred_element_type=jnp.float32)
        rotated = jnp.dot(stack(inward.astype(jnp.bfloat16)), right, preferred_element_type=jnp.float32)
        scaled = jnp.concatenate(
            [(rotated[q * A_DIM:(q + 1) * A_DIM] / damped).astype(jnp.bfloat16) for q in range(count)], axis=1
        )
        restored = jnp.dot(left, scaled, preferred_element_type=jnp.float32).astype(jnp.bfloat16)
        prepared = lax.dot_general(
            stack(restored), right, (((1,), (1,)), ((), ())), preferred_element_type=jnp.float32
        )
        for q in range(count):
            spread_ref[pl.ds(q, A_DIM, stride=count), :] = prepared[q * A_DIM:(q + 1) * A_DIM]
        for a in range(A_DIM):
            out_ref[rows, a * B_DIM:(a + 1) * B_DIM] = spread_ref[a * count:(a + 1) * count, :].astype(jnp.bfloat16)


def precondition(rows, *factors):
    operands = rows, *[pltpu.with_memory_space_constraint(m, pltpu.HBM) for m in factors]
    return pl.pallas_call(
        precondition_kernel,
        out_shape=jax.ShapeDtypeStruct(rows.shape, jnp.bfloat16),
        in_specs=[ANY_SPEC] * 4,
        out_specs=VMEM_SPEC,
        scratch_shapes=[pltpu.VMEM(m.shape, m.dtype) for m in operands]
        + [pltpu.VMEM((A_DIM * 16, B_DIM), jnp.float32)] * 2
        + [pltpu.SemaphoreType.DMA((4,))],
        compiler_params=pltpu.CompilerParams(vmem_limit_bytes=KERNEL_VMEM),
        cost_estimate=PREPARE_COST,
        name="precondition",
    )(*operands)


def owner_of(entry, chips):
    here = lax.axis_index("wide")
    arrival, side = entry // 2, entry % 2
    chip, core = lax.div(here, 2), lax.rem(here, 2)
    hop, crossed = (arrival + 1) // 2, (arrival + 1) % 2 if arrival else 0
    step = jnp.where(core == side, -hop, hop)
    ladder = chips == 8
    spot = jnp.where(lax.rem(chip, 2) == 0, lax.div(chip, 2), chips - 1 - lax.div(chip, 2)) if ladder else chip
    spot = lax.rem(spot + step + chips, chips)
    chip = jnp.where(spot < chips // 2, 2 * spot, 2 * chips - 1 - 2 * spot) if ladder else spot
    return 2 * chip + (1 - core if (side + crossed) % 2 else core)


def scores_kernel(entries, count, begin, first, last, query_ref, *refs):
    blocks, refs = refs[:count], refs[count:]
    if not first:
        total_ref, refs = refs[0], refs[1:]
    out_ref, sum_ref = refs[:2]
    height = sum(block.shape[0] for block in blocks) // len(entries)
    width = min(block.shape[1] for block in blocks)
    tile = column_tile(width)
    steps = width // tile
    missing = sum_ref.shape[1] - sum(block.shape[0] for block in blocks)
    chips = out_ref.shape[1] // height // 2
    if first:
        out_ref[...] = jnp.zeros_like(out_ref)

    def product(step):
        def columns(skipped):
            return pl.ds(pl.multiple_of(skipped + step * tile, LANES), tile)

        rows = [block[:, columns(begin if block.shape[1] > width else 0)] for block in blocks]
        if missing:
            rows.append(jnp.zeros((missing, tile), rows[0].dtype))
        return lax.dot_general(
            query_ref[:, columns(begin)], jnp.concatenate(rows, axis=0), (((1,), (1,)), ((), ())),
            preferred_element_type=jnp.float32,
        )

    sum_ref[...] = product(0)
    if steps > 1:
        @pl.loop(1, steps)
        def _(step):
            sum_ref[...] += product(step)

    per_tile = LANES // height
    owners = [owner_of(entry, chips) for entry in entries]

    def add(target_ref, rows):
        place = lax.broadcasted_iota(jnp.int32, (rows.size, LANES), 1) // height
        for i, owner in enumerate(owners):
            spot = lax.rem(owner, per_tile)
            held = sum_ref[rows, i // per_tile * LANES:(i // per_tile + 1) * LANES]
            moved = pltpu.roll(held, lax.rem(spot - i % per_tile + per_tile, per_tile) * height, 1)
            lanes = pl.ds(pl.multiple_of(lax.div(owner, per_tile) * LANES, LANES), LANES)
            target_ref[rows, lanes] += jnp.where(place == spot, moved, 0.0)

    if not last:
        add(out_ref, pl.ds(0, out_ref.shape[0]))
        return
    result_ref, sems = refs[2:]
    size = out_ref.shape[0] // RESULT_PARTS
    copies = []
    for i in range(RESULT_PARTS):
        rows = pl.ds(i * size, size)
        result_ref[rows, :] = total_ref[rows, :]
        add(result_ref, rows)
        copies.append(pltpu.make_async_copy(result_ref.at[rows, :], out_ref.at[rows, :], sems.at[i]))
        copies[-1].start()
    for copy in copies:
        copy.wait()


def column_tile(width):
    return max(t for t in range(LANES, min(K_TILE, width) + 1, LANES) if width % t == 0)


def add_scores(total, queries, entries, blocks, train_count, begin=0, last=False):
    rows = queries.shape[0]
    first = total is None
    operands = [pltpu.with_memory_space_constraint(queries, pltpu.VMEM), *blocks] + ([] if first else [total])
    lanes = -(-sum(block.shape[0] for block in blocks) // LANES) * LANES
    result = [pltpu.VMEM((rows, train_count), jnp.float32), pltpu.SemaphoreType.DMA((RESULT_PARTS,))]
    return pl.pallas_call(
        functools.partial(scores_kernel, entries, len(blocks), begin, first, last),
        out_shape=jax.ShapeDtypeStruct((rows, train_count), jnp.float32),
        in_specs=[VMEM_SPEC] * len(operands),
        out_specs=ANY_SPEC if last else VMEM_SPEC,
        scratch_shapes=[pltpu.VMEM((rows, lanes), jnp.float32)] + (result if last else []),
        input_output_aliases={} if first or last else {len(operands) - 1: 0},
        compiler_params=pltpu.CompilerParams(vmem_limit_bytes=KERNEL_VMEM),
        cost_estimate=SCORE_COST,
        name="scores",
    )(*operands)


def cut_kernel(source_ref, *pieces):
    row, column = 0, 0
    for piece in pieces:
        height, width = piece.shape
        piece[...] = source_ref[row:row + height, column:column + width]
        row, column = (row + height) % source_ref.shape[0], (column + width) % source_ref.shape[1]


def cut(block, shapes):
    return pl.pallas_call(
        cut_kernel,
        out_shape=[jax.ShapeDtypeStruct(shape, block.dtype) for shape in shapes],
        in_specs=[VMEM_SPEC],
        out_specs=[VMEM_SPEC] * len(shapes),
        compiler_params=pltpu.CompilerParams(vmem_limit_bytes=KERNEL_VMEM),
        cost_estimate=CUT_COST,
        name="cut",
    )(block)


def join_kernel(*refs):
    *blocks, out_ref = refs
    row = 0
    for block in blocks:
        out_ref[row:row + block.shape[0], :] = block[...]
        row += block.shape[0]


def join(*blocks):
    rows = sum(block.shape[0] for block in blocks)
    return pl.pallas_call(
        join_kernel,
        out_shape=jax.ShapeDtypeStruct((rows, blocks[0].shape[1]), blocks[0].dtype),
        in_specs=[VMEM_SPEC] * len(blocks),
        out_specs=VMEM_SPEC,
        compiler_params=pltpu.CompilerParams(vmem_limit_bytes=KERNEL_VMEM),
        cost_estimate=CUT_COST,
        name="join",
    )(*blocks)


def per_device(queries, train_rows, left_basis, right_basis, eigenvalues):
    devices = lax.axis_size("wide")
    chips = devices // 2
    ring = chip_ring(chips)
    hops = chips // 2
    train_count = devices * train_rows.shape[0]
    height, width = train_rows.shape

    along = [
        (2 * ring[i] + core, 2 * ring[(i + (-1 if core else 1)) % chips] + core)
        for i in range(chips)
        for core in range(2)
    ]
    across = [(d, d ^ 1) for d in range(devices)]
    send = lambda block, pairs: lax.ppermute(block, "wide", pairs)

    def after(block, array):
        return lax.optimization_barrier((block, array))

    raw = train_rows
    factors = left_basis, right_basis, eigenvalues
    other = precondition(send(train_rows, across), *factors)
    train_rows, other = after(train_rows, other)
    own = precondition(train_rows, *factors)
    chains = [raw, other]
    blocks = [own, other]
    score = lambda total, arrivals, blocks, **kw: add_scores(
        total, queries, [e for a in arrivals for e in (2 * a, 2 * a + 1)], blocks, train_count, **kw
    )
    pairs = [[own, other]]
    groups = [[a, a + 1] for a in range(0, chips - 6, 2)] + [[chips - 6, chips - 5, chips - 4]]
    total = None
    for arrival in range(1, chips - 1):
        chain = (arrival + 1) % 2
        block = send(chains[chain], along)
        if groups[0][-1] == arrival - 2:
            total = score(total, groups[0], [block for a in groups[0] for block in pairs[a]])
            groups.pop(0)
            block, total = after(block, total)
        if arrival == 1:
            block = precondition(block, *factors)
        if groups and groups[0][-1] == arrival - 1:
            if total is None:
                pairs[0][0], block = after(pairs[0][0], block)
            else:
                total, block = after(total, block)
        chains[chain] = block
        halves = cut(block, [(height // 2, width)] * 2) if arrival == chips - 2 else [block]
        pairs.append([block] + [send(half, across) for half in halves])

    group = [chips - 3, chips - 2, chips - 1]
    widths = [width * part // sum(LAST_PARTS) for part in LAST_PARTS]
    begin = 0
    joined = join(*pairs[chips - 3])
    for i, piece in enumerate(cut(chains[0], [(height, w) for w in widths])):
        if i == 1:
            piece, block = after(piece, block)
            pairs[-2 if len(pairs) == chips else -1][0] = block
        last = i == len(widths) - 1
        part = send(piece, along)
        if i == 0:
            part, joined = after(part, joined)
        if i:
            total = score(total, group, blocks, begin=begin)
            begin += widths[i - 1]
            part, total = after(part, total)
        swapped = [part] if last else cut(part, [(height // 2, widths[i])] * 2)
        blocks = [joined] + pairs[chips - 2] + [part] + [send(piece, across) for piece in swapped]
    return score(total, group, blocks, begin=begin, last=True)


def solution(mesh):
    in_specs = (P(("grp", "wide"), None), P(("grp", "wide"), None), P(), P(), P())
    out_specs = P(("grp", "wide"), None)
    return jax.shard_map(
        per_device, mesh=mesh, in_specs=in_specs, out_specs=out_specs, check_vma=False
    )
```

```python
import functools

import jax
import jax.numpy as jnp
from jax import lax
from jax.experimental import pallas as pl
from jax.experimental.pallas import tpu as pltpu
from jax.sharding import PartitionSpec as P

A_DIM = 128
B_DIM = 128
LANES = 128
K_TILE = 12288
RESULT_PARTS = 4
KERNEL_VMEM = 16 << 20
PREPARE_COST = pl.CostEstimate(flops=1, bytes_accessed=1, transcendentals=0)
SCORE_COST = pl.CostEstimate(flops=1, bytes_accessed=1, transcendentals=0)
CUT_COST = pl.CostEstimate(flops=1, bytes_accessed=1, transcendentals=0)
LAST_PARTS = 21, 11
ANY_SPEC = pl.BlockSpec(memory_space=pl.ANY)
VMEM_SPEC = pl.BlockSpec(memory_space=pltpu.VMEM)

DAMPING = 0.1


def chip_ring(chips):
    if chips == 8:
        return list(range(0, chips, 2)) + list(range(chips - 1, 0, -2))
    return list(range(chips))


def precondition_kernel(*refs):
    sources, out_ref, arrived = refs[:4], refs[4], refs[5:9]
    gather_ref, spread_ref, sems = refs[9:]
    fetches = [pltpu.make_async_copy(a, b, sems.at[i]) for i, (a, b) in enumerate(zip(sources, arrived))]
    for fetch in fetches:
        fetch.start()
    for fetch in fetches:
        fetch.wait()
    rows_ref, left_ref, right_ref, eig_ref = arrived
    count = gather_ref.shape[0] // A_DIM
    left = left_ref[...]
    right = right_ref[...]
    damped = eig_ref[...] + DAMPING

    def stack(wide):
        return jnp.concatenate([wide[:, q * B_DIM:(q + 1) * B_DIM] for q in range(count)], axis=0)

    for base in range(0, rows_ref.shape[0], count):
        rows = slice(base, base + count)
        for a in range(A_DIM):
            gather_ref[a * count:(a + 1) * count, :] = rows_ref[rows, a * B_DIM:(a + 1) * B_DIM].astype(jnp.float32)
        matrix = jnp.concatenate(
            [gather_ref[pl.ds(q, A_DIM, stride=count), :].astype(jnp.bfloat16) for q in range(count)], axis=1
        )
        inward = lax.dot_general(left, matrix, (((0,), (0,)), ((), ())), preferred_element_type=jnp.float32)
        rotated = jnp.dot(stack(inward.astype(jnp.bfloat16)), right, preferred_element_type=jnp.float32)
        scaled = jnp.concatenate(
            [(rotated[q * A_DIM:(q + 1) * A_DIM] / damped).astype(jnp.bfloat16) for q in range(count)], axis=1
        )
        restored = jnp.dot(left, scaled, preferred_element_type=jnp.float32).astype(jnp.bfloat16)
        prepared = lax.dot_general(
            stack(restored), right, (((1,), (1,)), ((), ())), preferred_element_type=jnp.float32
        )
        for q in range(count):
            spread_ref[pl.ds(q, A_DIM, stride=count), :] = prepared[q * A_DIM:(q + 1) * A_DIM]
        for a in range(A_DIM):
            out_ref[rows, a * B_DIM:(a + 1) * B_DIM] = spread_ref[a * count:(a + 1) * count, :].astype(jnp.bfloat16)


def precondition(rows, *factors):
    operands = rows, *[pltpu.with_memory_space_constraint(m, pltpu.HBM) for m in factors]
    return pl.pallas_call(
        precondition_kernel,
        out_shape=jax.ShapeDtypeStruct(rows.shape, jnp.bfloat16),
        in_specs=[ANY_SPEC] * 4,
        out_specs=VMEM_SPEC,
        scratch_shapes=[pltpu.VMEM(m.shape, m.dtype) for m in operands]
        + [pltpu.VMEM((A_DIM * 16, B_DIM), jnp.float32)] * 2
        + [pltpu.SemaphoreType.DMA((4,))],
        compiler_params=pltpu.CompilerParams(vmem_limit_bytes=KERNEL_VMEM),
        cost_estimate=PREPARE_COST,
        name="precondition",
    )(*operands)


def owner_of(entry, chips):
    here = lax.axis_index("wide")
    arrival, side = entry // 2, entry % 2
    chip, core = lax.div(here, 2), lax.rem(here, 2)
    hop, crossed = (arrival + 1) // 2, (arrival + 1) % 2 if arrival else 0
    step = jnp.where(core == side, -hop, hop)
    ladder = chips == 8
    spot = jnp.where(lax.rem(chip, 2) == 0, lax.div(chip, 2), chips - 1 - lax.div(chip, 2)) if ladder else chip
    spot = lax.rem(spot + step + chips, chips)
    chip = jnp.where(spot < chips // 2, 2 * spot, 2 * chips - 1 - 2 * spot) if ladder else spot
    return 2 * chip + (1 - core if (side + crossed) % 2 else core)


def scores_kernel(entries, count, begin, first, stage, query_ref, *refs):
    blocks, refs = refs[:count], refs[count:]
    if not first:
        total_ref, refs = refs[0], refs[1:]
    if stage == "close":
        begun_ref, refs = refs[0], refs[1:]
    out_ref = refs[0]
    sum_ref = out_ref if stage == "open" else refs[1]
    height = sum(block.shape[0] for block in blocks) // len(entries)
    width = min(block.shape[1] for block in blocks)
    tile = column_tile(width)
    steps = width // tile
    missing = sum_ref.shape[1] - sum(block.shape[0] for block in blocks)
    if first and stage is None:
        out_ref[...] = jnp.zeros_like(out_ref)

    def product(step):
        def columns(skipped):
            return pl.ds(pl.multiple_of(skipped + step * tile, LANES), tile)

        rows = [block[:, columns(begin if block.shape[1] > width else 0)] for block in blocks]
        if missing:
            rows.append(jnp.zeros((missing, tile), rows[0].dtype))
        return lax.dot_general(
            query_ref[:, columns(begin)], jnp.concatenate(rows, axis=0), (((1,), (1,)), ((), ())),
            preferred_element_type=jnp.float32,
        )

    sum_ref[...] = begun_ref[...] + product(0) if stage == "close" else product(0)
    if steps > 1:
        @pl.loop(1, steps)
        def _(step):
            sum_ref[...] += product(step)

    if stage == "open":
        return
    per_tile = LANES // height
    chips = out_ref.shape[1] // height // 2
    owners = [owner_of(entry, chips) for entry in entries]

    def add(target_ref, rows):
        place = lax.broadcasted_iota(jnp.int32, (rows.size, LANES), 1) // height
        for i, owner in enumerate(owners):
            spot = lax.rem(owner, per_tile)
            held = sum_ref[rows, i // per_tile * LANES:(i // per_tile + 1) * LANES]
            moved = pltpu.roll(held, lax.rem(spot - i % per_tile + per_tile, per_tile) * height, 1)
            lanes = pl.ds(pl.multiple_of(lax.div(owner, per_tile) * LANES, LANES), LANES)
            target_ref[rows, lanes] += jnp.where(place == spot, moved, 0.0)

    if stage is None:
        add(out_ref, pl.ds(0, out_ref.shape[0]))
        return
    result_ref, sems = refs[2:]
    size = out_ref.shape[0] // RESULT_PARTS
    copies = []
    for i in range(RESULT_PARTS):
        rows = pl.ds(i * size, size)
        result_ref[rows, :] = total_ref[rows, :]
        add(result_ref, rows)
        copies.append(pltpu.make_async_copy(result_ref.at[rows, :], out_ref.at[rows, :], sems.at[i]))
        copies[-1].start()
    for copy in copies:
        copy.wait()


def column_tile(width):
    return max(t for t in range(LANES, min(K_TILE, width) + 1, LANES) if width % t == 0)


def add_scores(total, queries, entries, blocks, train_count, begin=0, stage=None, begun=None):
    rows = queries.shape[0]
    first = total is None
    lanes = -(-sum(block.shape[0] for block in blocks) // LANES) * LANES
    operands = [pltpu.with_memory_space_constraint(queries, pltpu.VMEM), *blocks]
    operands += [array for array in (total, begun) if array is not None]
    scratch = [pltpu.VMEM((rows, lanes), jnp.float32)] if stage != "open" else []
    if stage == "close":
        scratch += [pltpu.VMEM((rows, train_count), jnp.float32), pltpu.SemaphoreType.DMA((RESULT_PARTS,))]
    return pl.pallas_call(
        functools.partial(scores_kernel, entries, len(blocks), begin, first, stage),
        out_shape=jax.ShapeDtypeStruct((rows, lanes if stage == "open" else train_count), jnp.float32),
        in_specs=[VMEM_SPEC] * len(operands),
        out_specs=ANY_SPEC if stage == "close" else VMEM_SPEC,
        scratch_shapes=scratch,
        input_output_aliases={} if first or stage else {len(operands) - 1: 0},
        compiler_params=pltpu.CompilerParams(vmem_limit_bytes=KERNEL_VMEM),
        cost_estimate=SCORE_COST,
        name="scores",
    )(*operands)


def cut_kernel(source_ref, *pieces):
    row, column = 0, 0
    for piece in pieces:
        height, width = piece.shape
        piece[...] = source_ref[row:row + height, column:column + width]
        row, column = (row + height) % source_ref.shape[0], (column + width) % source_ref.shape[1]


def cut(block, shapes):
    return pl.pallas_call(
        cut_kernel,
        out_shape=[jax.ShapeDtypeStruct(shape, block.dtype) for shape in shapes],
        in_specs=[VMEM_SPEC],
        out_specs=[VMEM_SPEC] * len(shapes),
        compiler_params=pltpu.CompilerParams(vmem_limit_bytes=KERNEL_VMEM),
        cost_estimate=CUT_COST,
        name="cut",
    )(block)


def join_kernel(*refs):
    *blocks, out_ref = refs
    row = 0
    for block in blocks:
        out_ref[row:row + block.shape[0], :] = block[...]
        row += block.shape[0]


def join(*blocks):
    rows = sum(block.shape[0] for block in blocks)
    return pl.pallas_call(
        join_kernel,
        out_shape=jax.ShapeDtypeStruct((rows, blocks[0].shape[1]), blocks[0].dtype),
        in_specs=[VMEM_SPEC] * len(blocks),
        out_specs=VMEM_SPEC,
        compiler_params=pltpu.CompilerParams(vmem_limit_bytes=KERNEL_VMEM),
        cost_estimate=CUT_COST,
        name="join",
    )(*blocks)


def per_device(queries, train_rows, left_basis, right_basis, eigenvalues):
    devices = lax.axis_size("wide")
    chips = devices // 2
    ring = chip_ring(chips)
    hops = chips // 2
    train_count = devices * train_rows.shape[0]
    height, width = train_rows.shape

    along = [
        (2 * ring[i] + core, 2 * ring[(i + (-1 if core else 1)) % chips] + core)
        for i in range(chips)
        for core in range(2)
    ]
    across = [(d, d ^ 1) for d in range(devices)]
    send = lambda block, pairs: lax.ppermute(block, "wide", pairs)

    def after(block, array):
        return lax.optimization_barrier((block, array))

    raw = train_rows
    factors = left_basis, right_basis, eigenvalues
    other = precondition(send(train_rows, across), *factors)
    train_rows, other = after(train_rows, other)
    own = precondition(train_rows, *factors)
    chains = [raw, other]
    blocks = [own, other]
    score = lambda total, arrivals, blocks, **kw: add_scores(
        total, queries, [e for a in arrivals for e in (2 * a, 2 * a + 1)], blocks, train_count, **kw
    )
    pairs = [[own, other]]
    groups = [[a, a + 1] for a in range(0, chips - 6, 2)] + [[chips - 6, chips - 5, chips - 4]]
    total = None
    for arrival in range(1, chips - 2):
        chain = (arrival + 1) % 2
        block = send(chains[chain], along)
        if groups[0][-1] == arrival - 2:
            total = score(total, groups[0], [block for a in groups[0] for block in pairs[a]])
            groups.pop(0)
            block, total = after(block, total)
        if arrival == 1:
            block = precondition(block, *factors)
        if groups and groups[0][-1] == arrival - 1:
            if total is None:
                pairs[0][0], block = after(pairs[0][0], block)
            else:
                total, block = after(total, block)
        chains[chain] = block
        halves = cut(block, [(height // 2, width)] * 2) if arrival == chips - 3 else [block]
        pairs.append([block] + [send(half, across) for half in halves])

    group = [chips - 3, chips - 2, chips - 1]
    widths = [width * part // sum(LAST_PARTS) for part in LAST_PARTS]
    joined = join(*pairs[chips - 3])
    cuts = [cut(chains[chain], [(height, w) for w in widths]) for chain in (1, 0)]

    def crossed(block):
        return [send(half, across) for half in cut(block, [(height // 2, block.shape[1])] * 2)]

    early = send(cuts[0][0], along)
    total = score(total, groups[0], [block for a in groups[0] for block in pairs[a]])
    early, total = after(early, total)
    late = send(cuts[1][0], along)
    late, joined = after(late, joined)
    blocks = [joined, early, send(early, across), late] + crossed(late)
    source, early = after(cuts[0][1], early)
    blocks[1] = early
    early = send(source, along)
    source, late = after(cuts[1][1], late)
    blocks[3] = late
    late = send(source, along)
    blocks[3], early = after(blocks[3], early)
    begun = score(None, group, blocks, stage="open")
    late, begun = after(late, begun)
    blocks = [joined, early, send(early, across), late, send(late, across)]
    return score(total, group, blocks, begin=widths[0], stage="close", begun=begun)


def solution(mesh):
    in_specs = (P(("grp", "wide"), None), P(("grp", "wide"), None), P(), P(), P())
    out_specs = P(("grp", "wide"), None)
    return jax.shard_map(
        per_device, mesh=mesh, in_specs=in_specs, out_specs=out_specs, check_vma=False
    )
```
